32 devices in a mesh: groups: 2 (over x), expert: 16 (over z, y, core).
Axes of the slice: x: 2, y: 2, z: 4, core: 2. Of those that a mesh axis runs over, the one named last changes fastest.
Arguments:
- tokens: bfloat16 [384, 3584], P(('groups', 'expert')), parts along dimension 0, may hold values from -6 to 6
- expert_ids: int32 [384, 8], P(('groups', 'expert')), parts along dimension 0, may hold values from 0 to 15, all different within a row; in each aligned block of 12 rows (0 to 11, 12 to 23, ...) at most 8 rows name the same one
- gate_weights: float32 [384, 8], P(('groups', 'expert')), parts along dimension 0, may hold values from 0.1 to 1
- w_gate: bfloat16 [16, 3584, 2048], P('expert'), may hold values from -0.09375 to 0.09375
- w_up: bfloat16 [16, 3584, 2048], P('expert'), may hold values from -0.09375 to 0.09375
- w_down: bfloat16 [16, 2048, 3584], P('expert'), may hold values from -0.125 to 0.125
Outputs:
- moe_out: bfloat16 [384, 3584], P(('groups', 'expert')), parts along dimension 0
The draws below stay inside these ranges and needn't reach their ends.
There are 2 independent parts, one for each index of `groups`. The reference program is written for one: setup_inputs(seed, part) draws one part's arguments, and reference() takes and returns one part's arrays. A program takes and returns all parts, laid end to end along the dimension named above; an argument that names none is the same for every part. Nothing has to cross between parts.
Inputs may be any that keep to these rules, and one draw needn't show every extreme that they name: `expert_ids`: each row names 8 different experts. Within the rows of one block (one device's 12 tokens) no expert is named more than 8 times, and in every draw some expert is named exactly 8 times in some block.
All inputs are finite; a program needn't handle non-finite values.
Results may differ from the reference program's by a relative error of at most 0.005.
Values may be sent and summed in bfloat16 or wider, within the bound.
No kernel may reach another device: no remote copies, remote signals or barrier semaphores. Data moves between devices by JAX's collectives and lax.ppermute only.
A program may use at most 128 MiB of HBM per device.

```python
import math
import jax
import jax.numpy as jnp
import numpy as np
from jax import lax

D = 3584
FFE = 2048
EXPERTS = 16
TOP = 8
TOK_DEV = 12
CAP = 8
SHARDS = 1
TOKENS = 192
N_EXPERT = 16


def block_levels(key, extent, cuts, low, largest):
    level, own = 1.0, jax.random.fold_in(key, 6)
    for axis_at, shards_of in cuts:
        draws = jnp.exp(jax.random.uniform(jax.random.fold_in(own, axis_at), (shards_of,), jnp.float32, low / len(cuts), largest / len(cuts)))
        level = level * jnp.repeat(draws, extent[axis_at] // shards_of).reshape([-1 if axis == axis_at else 1 for axis in range(len(extent))])
    return level


def deal_out(stream_key, own, number, rows, count, top, most, lean):
    order = jax.random.permutation(stream_key, count)
    packed, common = load_shares(count, rows * top, most, lean, True), load_shares(count, rows * top, most, lean, False)
    places = jnp.arange(count)

    def named(sizes, turn):
        used = int((sizes > 0).sum())
        fixed = max(1, used // 4)
        passed = fixed + (places - fixed + turn * (used - fixed)) % max(1, count - fixed)
        return jnp.zeros((count,), jnp.int32).at[order[jnp.where(places < fixed, places, passed)]].set(jnp.asarray(sizes, jnp.int32))

    sizes = jnp.where(number % 4 == 0, named(packed, number // 4), named(common, number - number // 4 - 1))
    mixed = jax.random.permutation(jax.random.fold_in(own, 3), count)
    giver, taker = mixed[0:count // 2 * 2:2], mixed[1:count // 2 * 2:2]
    room = jnp.minimum(sizes[giver] - 1, most - sizes[taker]) // 2
    room = jnp.where((giver == order[0]) | (taker == order[0]) | (sizes[taker] == 0), 0, jnp.maximum(room, 0))
    passed = jax.random.randint(jax.random.fold_in(own, 4), (count // 2,), 0, 1 << 20) % (room + 1)
    sizes = sizes.at[giver].add(-passed).at[taker].add(passed)
    labels = jnp.searchsorted(jnp.cumsum(sizes), jnp.arange(rows * top), side="right").astype(jnp.int32)
    grid = labels.reshape(top, rows).T
    grid = grid[jax.random.permutation(jax.random.fold_in(own, 1), rows)]
    turn = jax.random.randint(jax.random.fold_in(own, 2), (rows, 1), 0, top)
    return jnp.take_along_axis(grid, (jnp.arange(top)[None, :] + turn) % top, axis=1)


def load_shares(number_of, total, reach, slope, full):
    portions = [(1 << 20) // math.isqrt(rank ** slope) + 1 for rank in range(1, number_of + 1)]
    largest = reach if full else min(reach, max(-(-total // number_of), total * portions[0] // sum(portions)))
    least = 1 if total - largest >= number_of - 1 else 0
    given, rest = [largest] + [least] * (number_of - 1), total - largest - least * (number_of - 1)
    while rest > 0:
        candidates = [i for i in range(1, number_of) if given[i] < largest] or [i for i in range(1, number_of) if given[i] < reach]
        whole, remaining = sum([portions[i] for i in candidates]), rest
        for i in candidates:
            addition = min(reach - given[i], max(1, remaining * portions[i] // whole), rest)
            given[i] = given[i] + addition
            rest = rest - addition
    return np.array(given)


def centred(rng, shape, spread, reach, split=(), kind=jnp.bfloat16):
    entries = jax.random.normal(rng, shape, jnp.float32) * spread
    if len(split) > 0:
        entries = block_levels(rng, shape, split, -0.22, 0.18) * entries
    return jnp.clip(entries, min=-reach, max=reach).astype(kind)


def setup_inputs(seed: int = 0, part: int = 0) -> dict:
    keys = jax.random.split(jax.random.key(seed), 7)
    part_splits = jax.random.split(jax.random.fold_in(keys[6], part), 7)
    tokens = centred(part_splits[0], (TOKENS, D), 1.0, 6.0, ((0, 16),))
    expert_ids_keys = jax.random.split(jax.random.fold_in(part_splits[1], 1), TOKENS // TOK_DEV)
    expert_ids_turns = jax.random.permutation(jax.random.fold_in(part_splits[1], 3), TOKENS // TOK_DEV)
    expert_ids = jax.vmap(lambda own, number: deal_out(jax.random.fold_in(part_splits[1], 2), own, number, TOK_DEV, EXPERTS, TOP, CAP, 2))(expert_ids_keys, expert_ids_turns).reshape((TOKENS, TOP))
    gate_weights = jnp.clip(jnp.exp(math.log(1.0) - 2.3025851 * jax.random.uniform(part_splits[2], (TOKENS, TOP), jnp.float32) ** block_levels(part_splits[2], (TOKENS, TOP), ((0, 16),), -0.2, 0.2)), 0.1, 1.0)
    w_gate = centred(keys[3], (EXPERTS * SHARDS, D, FFE // SHARDS), D ** -0.5, 0.09375, ((0, 16),))
    w_up = centred(keys[4], (EXPERTS * SHARDS, D, FFE // SHARDS), D ** -0.5, 0.09375, ((0, 16),))
    w_down = centred(keys[5], (EXPERTS * SHARDS, FFE // SHARDS, D), FFE ** -0.5, 0.125, ((0, 16),))
    return dict(tokens=tokens, expert_ids=expert_ids, gate_weights=gate_weights, w_gate=w_gate, w_up=w_up, w_down=w_down)


def slot_numbers(routed):
    chosen = (routed[..., None] == jnp.arange(EXPERTS, dtype=jnp.int32)).astype(jnp.int32)
    counts = jnp.sum(chosen, axis=2)
    before = jnp.cumsum(counts, axis=1) - counts
    return jnp.sum(chosen * before[:, :, None, :], axis=3)


def reference(tokens, expert_ids, gate_weights, w_gate, w_up, w_down):
    shards = N_EXPERT // EXPERTS
    slice_units = FFE // shards
    slot_index = slot_numbers(expert_ids.reshape(N_EXPERT, TOK_DEV, TOP)).reshape(TOKENS, TOP)
    block_of = (jnp.arange(TOKENS, dtype=jnp.int32) // TOK_DEV).astype(jnp.int32)
    gate_all = w_gate.reshape(shards, EXPERTS, D, slice_units)
    up_all = w_up.reshape(shards, EXPERTS, D, slice_units)
    down_all = w_down.reshape(shards, EXPERTS, slice_units, D)
    buffer_rows = N_EXPERT * CAP

    def one_expert(running, expert):
        chosen = expert_ids == expert
        is_used = jnp.any(chosen, axis=1)
        slot_e = jnp.sum(jnp.where(chosen, slot_index, 0), axis=1).astype(jnp.int32)
        target = jnp.where(is_used, block_of * CAP + slot_e, buffer_rows).astype(jnp.int32)
        buffer = jnp.zeros((buffer_rows, D), jnp.bfloat16).at[target].set(tokens, mode="drop")
        gate_full = jnp.transpose(gate_all[:, expert], (1, 0, 2)).reshape(D, FFE)
        up_full = jnp.transpose(up_all[:, expert], (1, 0, 2)).reshape(D, FFE)
        down_full = down_all[:, expert].reshape(FFE, D)
        gate_act = jnp.dot(buffer, gate_full, preferred_element_type=jnp.float32)
        up_act = jnp.dot(buffer, up_full, preferred_element_type=jnp.float32)
        hidden = (jax.nn.silu(gate_act) * up_act).astype(jnp.bfloat16)
        expert_rows = jnp.dot(hidden, down_full, preferred_element_type=jnp.float32)
        weight = jnp.sum(jnp.where(chosen, gate_weights, jnp.zeros_like(gate_weights)), axis=1)
        picked = expert_rows[jnp.minimum(target, buffer_rows - 1)] * weight[:, None]
        return running + picked, None

    summed_all, _ = lax.scan(one_expert, jnp.zeros((TOKENS, D), jnp.float32), jnp.arange(EXPERTS, dtype=jnp.int32))
    return summed_all.astype(jnp.bfloat16)
```

```python
import functools

import jax
import jax.numpy as jnp
from jax import lax
from jax.experimental import pallas as pl
from jax.experimental.pallas import tpu as pltpu
from jax.sharding import PartitionSpec as P

EXPERTS = 16
CAP = 8
LANES = 128
MIB = 1024 * 1024
BF16 = jnp.bfloat16
F32 = jnp.float32


def iota(shape, dim):
    return lax.broadcasted_iota(jnp.int32, shape, dim)


def pack_kernel(tokens_ref, ids_ref, weights_ref, out_ref):
    rows, width = tokens_ref.shape
    half = width // 2
    expert_of = lax.rem(iota((rows, LANES), 1), EXPERTS)
    kind = lax.div(iota((rows, LANES), 1), EXPERTS)
    chosen = jnp.zeros((rows, LANES), F32)
    weight = jnp.zeros((rows, LANES), F32)
    for j in range(ids_ref.shape[1]):
        same = ids_ref[:, j : j + 1] == expert_of
        chosen = chosen + jnp.where(same, 1.0, 0.0)
        weight = weight + jnp.where(same, weights_ref[:, j : j + 1], 0.0)
    rank = jnp.zeros((rows, LANES), F32)
    row_of = iota((rows, LANES), 0)
    for r in range(rows - 1):
        rank = rank + jnp.where(row_of > r, chosen[r : r + 1, :], 0.0)
    high = weight.astype(BF16).astype(F32)
    middle = (weight - high).astype(BF16).astype(F32)
    low = weight - high - middle
    routing = jnp.where(
        kind == 0,
        chosen * (rank + 1.0),
        jnp.where(kind == 1, high, jnp.where(kind == 2, middle, jnp.where(kind == 3, low, 0.0))),
    )
    tokens = tokens_ref[...].astype(F32)
    out_ref[:, :half] = jnp.concatenate([tokens[:, :half], tokens[:, half:]], axis=0).astype(BF16)
    out_ref[:, half:] = jnp.concatenate([routing, routing], axis=0).astype(BF16)


def expert_kernel(rows, parts, *refs):
    packed_refs, (gate_hbm, up_hbm, down_hbm) = refs[:parts], refs[parts : parts + 3]
    keep_ref, send_ref = refs[parts + 3 : parts + 5]
    packed, x, hidden, gate, up, down, sems = refs[parts + 5 :]
    width, units = gate.shape
    half = width // 2
    tile = 512 if units % 512 == 0 else units
    in_steps, out_steps = units // tile, half // 256

    def copies():
        for i in range(in_steps):
            cols = pl.ds(i * tile, tile)
            yield pltpu.make_async_copy(gate_hbm.at[:, cols], gate.at[:, cols], sems.at[2 * i])
            yield pltpu.make_async_copy(up_hbm.at[:, cols], up.at[:, cols], sems.at[2 * i + 1])
        yield pltpu.make_async_copy(down_hbm.at[:, :half], down.at[:, :half], sems.at[2 * in_steps])
        yield pltpu.make_async_copy(down_hbm.at[:, half:], down.at[:, half:], sems.at[2 * in_steps + 1])

    pending = list(copies())
    for copy in pending:
        copy.start()

    at = 0
    for ref in packed_refs:
        packed[at : at + ref.shape[0], :] = ref[...]
        at += ref.shape[0]
    count = packed.shape[0]
    slots = x.shape[0]
    expert = lax.rem(lax.axis_index("expert"), EXPERTS)
    routing = packed[:, half:]
    pick_row = jnp.where(iota((slots, LANES), 1) == expert, 1.0, 0.0).astype(BF16)
    rank_row = lax.dot_general(pick_row, routing, (((1,), (1,)), ((), ())), preferred_element_type=F32)
    pick_col = jnp.where(iota((LANES, slots), 0) == expert, 1.0, 0.0).astype(BF16)
    rank_col = jnp.dot(routing, pick_col, preferred_element_type=F32)

    def table(rank, packed_dim, slot_dim):
        at = iota(rank.shape, packed_dim)
        block = lax.div(at, 2 * rows)
        second = (at - block * (2 * rows)) >= rows
        hit = (rank > 0) & (iota(rank.shape, slot_dim) == block * CAP + rank.astype(jnp.int32) - 1)
        one = jnp.where(hit, 1.0, 0.0)
        return (jnp.where(second, 0.0, one).astype(BF16), jnp.where(second, one, 0.0).astype(BF16))

    left, right = table(rank_row, 1, 0)
    x[:, :half] = jnp.dot(left, packed[:, :half], preferred_element_type=F32).astype(BF16)
    x[:, half:] = jnp.dot(right, packed[:, :half], preferred_element_type=F32).astype(BF16)
    slot_routing = jnp.dot(left, routing, preferred_element_type=F32)
    lane = iota(slot_routing.shape, 1)
    is_weight = (lax.rem(lane, EXPERTS) == expert) & (lane >= EXPERTS) & (lane < 4 * EXPERTS)
    weight = jnp.sum(jnp.where(is_weight, slot_routing, 0.0), axis=1, keepdims=True)

    for i in range(in_steps):
        cols = slice(i * tile, (i + 1) * tile)
        pending[2 * i].wait()
        gate_act = jnp.dot(x[...], gate[:, cols], preferred_element_type=F32)
        pending[2 * i + 1].wait()
        up_act = jnp.dot(x[...], up[:, cols], preferred_element_type=F32)
        hidden[:, cols] = (gate_act / (1.0 + jnp.exp(-gate_act)) * up_act).astype(BF16)
    back_left, back_right = table(rank_col, 0, 1)
    back = jnp.concatenate([back_left, back_right], axis=1)
    pending[2 * in_steps].wait()
    pending[2 * in_steps + 1].wait()
    for i in range(out_steps):
        cols = slice(i * 256, (i + 1) * 256)
        both = []
        for s in range(2):
            act = jnp.dot(hidden[...], down[:, s * half + i * 256 : s * half + (i + 1) * 256], preferred_element_type=F32)
            both.append((act * weight).astype(BF16))
        spread = jnp.dot(back, jnp.concatenate(both, axis=0), preferred_element_type=F32).astype(BF16)
        keep_ref[:, cols] = spread[: count // 2]
        send_ref[:, cols] = spread[count // 2 :]


def body(tokens, expert_ids, gate_weights, w_gate, w_up, w_down):
    size = lax.axis_size("expert")
    steps = size // 4
    rows, width = tokens.shape
    units = w_gate.shape[2]
    half = width // 2
    block = 2 * rows

    def send(x, pairs):
        return lax.ppermute(x, "expert", pairs)

    flip_core = [(i, i ^ 1) for i in range(size)]
    flip_second = [(i, i ^ 2) for i in range(size)]

    def shift(s):
        return [(i, (i + 4 * s) % size) for i in range(size)]

    own = pl.pallas_call(
        pack_kernel,
        out_shape=jax.ShapeDtypeStruct((block, half + LANES), BF16),
        name="pack",
    )(tokens, expert_ids, gate_weights)
    shifted = [send(own, shift(s)) for s in range(1, steps)]
    across = send(own, flip_second)
    column = jnp.concatenate([own] + shifted, axis=0)
    plane = jnp.concatenate([column, across, send(column[block:], flip_second)], axis=0)
    other = send(plane, flip_core)

    count = size * block
    slots = size * CAP
    any_space = pl.BlockSpec(memory_space=pl.ANY)
    vmem = pl.BlockSpec(memory_space=pltpu.VMEM)
    keep, away = pl.pallas_call(
        functools.partial(expert_kernel, rows, 2),
        out_shape=[jax.ShapeDtypeStruct((count // 2, half), BF16)] * 2,
        in_specs=[vmem] * 2 + [any_space] * 3,
        out_specs=[vmem] * 2,
        scratch_shapes=[
            pltpu.VMEM((count, half + LANES), BF16),
            pltpu.VMEM((slots, width), BF16),
            pltpu.VMEM((slots, units), BF16),
            pltpu.VMEM((width, units), BF16),
            pltpu.VMEM((width, units), BF16),
            pltpu.VMEM((units, width), BF16),
            pltpu.SemaphoreType.DMA((16,)),
        ],
        compiler_params=pltpu.CompilerParams(vmem_limit_bytes=60 * MIB),
        cost_estimate=pl.CostEstimate(
            flops=6 * slots * width * units, bytes_accessed=6 * width * units, transcendentals=slots * units
        ),
        name="experts",
    )(plane, other, w_gate[0], w_up[0], w_down[0])

    def add(a, b):
        return (a.astype(F32) + b.astype(F32)).astype(BF16)

    chip = add(keep, send(away, flip_core))
    line = add(chip[: count // 4], send(chip[count // 4 :], flip_second))
    total = line[:block].astype(F32)
    for s in range(1, steps):
        total = total + send(line[s * block : (s + 1) * block], shift(size // 4 - s)).astype(F32)
    total = total.astype(BF16)
    return jnp.concatenate([total[:rows], total[rows:]], axis=1)


def solution(mesh):
    return jax.shard_map(
        body,
        mesh=mesh,
        in_specs=(
            P(("groups", "expert"), None),
            P(("groups", "expert"), None),
            P(("groups", "expert"), None),
            P("expert", None, None),
            P("expert", None, None),
            P("expert", None, None),
        ),
        out_specs=P(("groups", "expert"), None),
        check_vma=False,
    )
```

```python
import functools

import jax
import jax.numpy as jnp
from jax import lax
from jax.experimental import pallas as pl
from jax.experimental.pallas import tpu as pltpu
from jax.sharding import PartitionSpec as P

EXPERTS = 16
CAP = 8
LANES = 128
CHUNKS = 2
MIB = 1024 * 1024
BF16 = jnp.bfloat16
F32 = jnp.float32
IN_VMEM = pl.BlockSpec(memory_space=pltpu.VMEM)
ANYWHERE = pl.BlockSpec(memory_space=pl.ANY)


def iota(shape, dim):
    return lax.broadcasted_iota(jnp.int32, shape, dim)


def near(x):
    return pltpu.with_memory_space_constraint(x, pltpu.VMEM)


def far(x):
    return pltpu.with_memory_space_constraint(x, pltpu.HBM)


def pack_kernel(tokens_ref, ids_ref, weights_ref, out_ref):
    rows, width = tokens_ref.shape
    half = width // 2
    ids = ids_ref[...].T
    weights = weights_ref[...].T
    expert_of = lax.rem(iota((rows, LANES), 1), EXPERTS)
    kind = lax.div(iota((rows, LANES), 1), EXPERTS)
    chosen = jnp.zeros((rows, LANES), F32)
    weight = jnp.zeros((rows, LANES), F32)
    for j in range(ids.shape[1]):
        same = ids[:, j : j + 1] == expert_of
        chosen = chosen + jnp.where(same, 1.0, 0.0)
        weight = weight + jnp.where(same, weights[:, j : j + 1], 0.0)
    rank = jnp.zeros((rows, LANES), F32)
    row_of = iota((rows, LANES), 0)
    for r in range(rows - 1):
        rank = rank + jnp.where(row_of > r, chosen[r : r + 1, :], 0.0)
    high = weight.astype(BF16).astype(F32)
    middle = (weight - high).astype(BF16).astype(F32)
    low = weight - high - middle
    routing = jnp.where(
        kind == 0,
        chosen * (rank + 1.0),
        jnp.where(kind == 1, high, jnp.where(kind == 2, middle, jnp.where(kind == 3, low, 0.0))),
    )
    tokens = tokens_ref[...].astype(F32)
    out_ref[:, :half] = jnp.concatenate([tokens[:, :half], tokens[:, half:]], axis=0).astype(BF16)
    out_ref[:, half:] = jnp.concatenate([routing, routing], axis=0).astype(BF16)


def load_kernel(spans, w_ref, *refs):
    out_ref, sems = refs[-2:]
    copies, at = [], 0
    for i, (begin, size) in enumerate(spans):
        copies.append(
            pltpu.make_async_copy(w_ref.at[:, pl.ds(begin, size)], out_ref.at[:, pl.ds(at, size)], sems.at[i])
        )
        at += size
    for copy in copies:
        copy.start()
    for copy in copies:
        copy.wait()


def load(w, spans, *after):
    size = sum(s for _, s in spans)
    return pl.pallas_call(
        functools.partial(load_kernel, spans),
        out_shape=pltpu.VMEM((w.shape[0], size), w.dtype),
        in_specs=[ANYWHERE] * (1 + len(after)),
        out_specs=IN_VMEM,
        scratch_shapes=[pltpu.SemaphoreType.DMA((len(spans),))],
        compiler_params=pltpu.CompilerParams(vmem_limit_bytes=MIB),
        cost_estimate=pl.CostEstimate(flops=0, bytes_accessed=4 * w.shape[0] * size, transcendentals=0),
        name="load",
    )(far(w), *after)


def project(hidden, down, weight, back, keep_ref, send_ref):
    span = keep_ref.shape[1]
    act = jnp.dot(hidden, down[...], preferred_element_type=F32)
    act = (act * weight).astype(BF16)
    both = jnp.concatenate([act[:, :span], act[:, span:]], axis=0)
    spread = jnp.dot(back, both, preferred_element_type=F32).astype(BF16)
    keep_ref[...] = spread[: keep_ref.shape[0]]
    send_ref[...] = spread[keep_ref.shape[0] :]


def expert_kernel(rows, planes, gates, spans, *refs):
    plane_refs, refs = refs[:planes], refs[planes:]
    gate_refs, up_refs, down_hbm, refs = refs[:gates], refs[gates : 2 * gates], refs[2 * gates], refs[2 * gates + 1 :]
    keep_ref, send_ref, hidden, weight_ref, back_ref, later_refs, x, down, sems = (*refs[:5], refs[5:-3], *refs[-3:])
    half = x.shape[1] // 2
    slots = x.shape[0]
    copies = []
    for i, (begin, size) in enumerate(spans):
        target = (down, *later_refs)[i // 2].at[:, pl.ds(i % 2 * size, size)]
        copies.append(pltpu.make_async_copy(down_hbm.at[:, pl.ds(begin, size)], target, sems.at[i]))
    for copy in copies:
        copy.start()

    expert = lax.rem(lax.axis_index("expert"), EXPERTS)
    pick_row = jnp.where(iota((slots, LANES), 1) == expert, 1.0, 0.0).astype(BF16)
    pick_col = jnp.where(iota((LANES, slots), 0) == expert, 1.0, 0.0).astype(BF16)

    def table(rank, packed_dim, slot_dim, first):
        at = iota(rank.shape, packed_dim) + first
        block = lax.div(at, 2 * rows)
        second = (at - block * (2 * rows)) >= rows
        hit = (rank > 0) & (iota(rank.shape, slot_dim) == block * CAP + rank.astype(jnp.int32) - 1)
        one = jnp.where(hit, 1.0, 0.0)
        return (jnp.where(second, 0.0, one).astype(BF16), jnp.where(second, one, 0.0).astype(BF16))

    first, left_x, right_x, slot_routing = 0, 0.0, 0.0, 0.0
    for ref in plane_refs:
        count = ref.shape[0]
        routing = ref[:, half:]
        rank_row = lax.dot_general(pick_row, routing, (((1,), (1,)), ((), ())), preferred_element_type=F32)
        rank_col = jnp.dot(routing, pick_col, preferred_element_type=F32)
        left, right = table(rank_row, 1, 0, first)
        back_left, back_right = table(rank_col, 0, 1, first)
        back_ref[first : first + count, :slots] = back_left
        back_ref[first : first + count, slots:] = back_right
        left_x = left_x + jnp.dot(left, ref[:, :half], preferred_element_type=F32)
        right_x = right_x + jnp.dot(right, ref[:, :half], preferred_element_type=F32)
        slot_routing = slot_routing + jnp.dot(left, routing, preferred_element_type=F32)
        first += count
    x[:, :half] = left_x.astype(BF16)
    x[:, half:] = right_x.astype(BF16)
    lane = iota(slot_routing.shape, 1)
    is_weight = (lax.rem(lane, EXPERTS) == expert) & (lane >= EXPERTS) & (lane < 4 * EXPERTS)
    weight = jnp.sum(jnp.where(is_weight, slot_routing, 0.0), axis=1, keepdims=True)
    weight_ref[...] = jnp.broadcast_to(weight, weight_ref.shape)

    at = 0
    for gate_ref, up_ref in zip(gate_refs, up_refs):
        units = gate_ref.shape[1]
        tile = 512 if units % 512 == 0 else units
        for i in range(units // tile):
            cols = slice(i * tile, (i + 1) * tile)
            gate_act = jnp.dot(x[...], gate_ref[:, cols], preferred_element_type=F32)
            up_act = jnp.dot(x[...], up_ref[:, cols], preferred_element_type=F32)
            hidden[:, at : at + tile] = (gate_act / (1.0 + jnp.exp(-gate_act)) * up_act).astype(BF16)
            at += tile
    for copy in copies[:2]:
        copy.wait()
    project(hidden[...], down, weight, back_ref[...], keep_ref, send_ref)
    for copy in copies[2:]:
        copy.wait()


def project_kernel(hidden, weight_ref, back, down, keep_ref, send_ref):
    project(hidden[...], down, weight_ref[:, :1], back[...], keep_ref, send_ref)


def body(tokens, expert_ids, gate_weights, w_gate, w_up, w_down):
    size = lax.axis_size("expert")
    steps = size // 4
    rows, width = tokens.shape
    units = w_gate.shape[2]
    half = width // 2
    block = 2 * rows
    count = size * block
    slots = size * CAP
    span = half // CHUNKS

    def send(x, pairs):
        return lax.ppermute(x, "expert", pairs)

    flip_core = [(i, i ^ 1) for i in range(size)]
    flip_second = [(i, i ^ 2) for i in range(size)]

    def shift(s):
        return [(i, (i + 4 * s) % size) for i in range(size)]

    own = pl.pallas_call(
        pack_kernel,
        out_shape=pltpu.VMEM((block, half + LANES), BF16),
        name="pack",
    )(tokens, expert_ids.T, gate_weights.T)
    low, high = [(0, units // 2)], [(units // 2, units // 2)]
    gates, ups = [load(w_gate[0], low)], [load(w_up[0], low)]
    spans = [(c * span + h * half, span) for c in range(CHUNKS) for h in range(2)]

    shifted = [send(own, shift(s)) for s in range(1, steps)]
    across = send(own, flip_second)
    column = jnp.concatenate([own] + shifted, axis=0)
    onward, gates[0], ups[0] = lax.optimization_barrier((column[block:], gates[0], ups[0]))
    plane = jnp.concatenate([column, across, send(onward, flip_second)], axis=0)
    gates.append(load(w_gate[0], high, onward))
    ups.append(load(w_up[0], high, onward))
    plane, gates[1], ups[1] = lax.optimization_barrier((plane, gates[1], ups[1]))
    other = send(plane, flip_core)

    outs = [pltpu.VMEM((count // 2, span), BF16)] * 2
    keep, away, hidden, weight, back, *downs = pl.pallas_call(
        functools.partial(expert_kernel, rows, 2, len(gates), spans),
        out_shape=outs
        + [
            pltpu.VMEM((slots, units), BF16),
            pltpu.VMEM((slots, LANES), F32),
            pltpu.VMEM((count, 2 * slots), BF16),
        ]
        + [pltpu.VMEM((units, 2 * span), BF16)] * (CHUNKS - 1),
        in_specs=[IN_VMEM] * (2 + 2 * len(gates)) + [ANYWHERE],
        out_specs=[IN_VMEM] * (4 + CHUNKS),
        scratch_shapes=[
            pltpu.VMEM((slots, width), BF16),
            pltpu.VMEM((units, 2 * span), BF16),
            pltpu.SemaphoreType.DMA((len(spans),)),
        ],
        compiler_params=pltpu.CompilerParams(vmem_limit_bytes=14 * MIB),
        cost_estimate=pl.CostEstimate(
            flops=5 * slots * width * units, bytes_accessed=4 * width * units, transcendentals=slots * units
        ),
        name="experts",
    )(near(plane), near(other), *gates, *ups, far(w_down[0]))
    results = [(keep, away)]
    for down in downs:
        results.append(
            pl.pallas_call(
                project_kernel,
                out_shape=outs,
                in_specs=[IN_VMEM] * 4,
                out_specs=[IN_VMEM] * 2,
                compiler_params=pltpu.CompilerParams(vmem_limit_bytes=14 * MIB),
                cost_estimate=pl.CostEstimate(
                    flops=slots * width * units, bytes_accessed=width * units, transcendentals=0
                ),
                name="project",
            )(hidden, weight, back, down)
        )

    def add(a, b):
        return (a.astype(F32) + b.astype(F32)).astype(BF16)

    totals = []
    for keep, away in results:
        chip = add(keep, send(away, flip_core))
        line = add(chip[: count // 4], send(chip[count // 4 :], flip_second))
        total = line[:block].astype(F32)
        for s in range(1, steps):
            total = total + send(line[s * block : (s + 1) * block], shift(steps - s)).astype(F32)
        totals.append(total.astype(BF16))
    return jnp.concatenate([t[:rows] for t in totals] + [t[rows:] for t in totals], axis=1)


def solution(mesh):
    return jax.shard_map(
        body,
        mesh=mesh,
        in_specs=(
            P(("groups", "expert"), None),
            P(("groups", "expert"), None),
            P(("groups", "expert"), None),
            P("expert", None, None),
            P("expert", None, None),
            P("expert", None, None),
        ),
        out_specs=P(("groups", "expert"), None),
        check_vma=False,
    )
```

```python
import functools

import jax
import jax.numpy as jnp
from jax import lax
from jax.experimental import pallas as pl
from jax.experimental.pallas import tpu as pltpu
from jax.sharding import PartitionSpec as P

EXPERTS = 16
CAP = 8
LANES = 128
CHUNKS = 2
MIB = 1024 * 1024
BF16 = jnp.bfloat16
F32 = jnp.float32
IN_VMEM = pl.BlockSpec(memory_space=pltpu.VMEM)
ANYWHERE = pl.BlockSpec(memory_space=pl.ANY)


def iota(shape, dim):
    return lax.broadcasted_iota(jnp.int32, shape, dim)


def near(x):
    return pltpu.with_memory_space_constraint(x, pltpu.VMEM)


def far(x):
    return pltpu.with_memory_space_constraint(x, pltpu.HBM)


def pack_kernel(tokens_ref, ids_ref, weights_ref, out_ref):
    rows, width = tokens_ref.shape
    half = width // 2
    ids = ids_ref[...].T
    weights = weights_ref[...].T
    expert_of = lax.rem(iota((rows, LANES), 1), EXPERTS)
    kind = lax.div(iota((rows, LANES), 1), EXPERTS)
    chosen = jnp.zeros((rows, LANES), F32)
    weight = jnp.zeros((rows, LANES), F32)
    for j in range(ids.shape[1]):
        same = ids[:, j : j + 1] == expert_of
        chosen = chosen + jnp.where(same, 1.0, 0.0)
        weight = weight + jnp.where(same, weights[:, j : j + 1], 0.0)
    rank = jnp.zeros((rows, LANES), F32)
    row_of = iota((rows, LANES), 0)
    for r in range(rows - 1):
        rank = rank + jnp.where(row_of > r, chosen[r : r + 1, :], 0.0)
    high = weight.astype(BF16).astype(F32)
    middle = (weight - high).astype(BF16).astype(F32)
    low = weight - high - middle
    routing = jnp.where(
        kind == 0,
        chosen * (rank + 1.0),
        jnp.where(kind == 1, high, jnp.where(kind == 2, middle, jnp.where(kind == 3, low, 0.0))),
    )
    tokens = tokens_ref[...].astype(F32)
    out_ref[:, :half] = jnp.concatenate([tokens[:, :half], tokens[:, half:]], axis=0).astype(BF16)
    out_ref[:, half:] = jnp.concatenate([routing, routing], axis=0).astype(BF16)


def load_kernel(spans, w_ref, *refs):
    out_ref, sems = refs[-2:]
    copies, at = [], 0
    for i, (begin, size) in enumerate(spans):
        copies.append(
            pltpu.make_async_copy(w_ref.at[:, pl.ds(begin, size)], out_ref.at[:, pl.ds(at, size)], sems.at[i])
        )
        at += size
    for copy in copies:
        copy.start()
    for copy in copies:
        copy.wait()


def load(w, spans, *after):
    size = sum(s for _, s in spans)
    return pl.pallas_call(
        functools.partial(load_kernel, spans),
        out_shape=pltpu.VMEM((w.shape[0], size), w.dtype),
        in_specs=[ANYWHERE] * (1 + len(after)),
        out_specs=IN_VMEM,
        scratch_shapes=[pltpu.SemaphoreType.DMA((len(spans),))],
        compiler_params=pltpu.CompilerParams(vmem_limit_bytes=MIB),
        cost_estimate=pl.CostEstimate(flops=0, bytes_accessed=4 * w.shape[0] * size, transcendentals=0),
        name="load",
    )(far(w), *after)


def project(hidden, down, weight, back, keep_ref, send_ref):
    span = keep_ref.shape[1]
    act = jnp.dot(hidden, down[...], preferred_element_type=F32)
    act = (act * weight).astype(BF16)
    both = jnp.concatenate([act[:, :span], act[:, span:]], axis=0)
    spread = jnp.dot(back, both, preferred_element_type=F32).astype(BF16)
    keep_ref[...] = spread[: keep_ref.shape[0]]
    send_ref[...] = spread[keep_ref.shape[0] :]


def expert_kernel(rows, planes, gates, spans, *refs):
    plane_refs, refs = refs[:planes], refs[planes:]
    gate_refs, up_refs, down_hbm, refs = refs[:gates], refs[gates : 2 * gates], refs[2 * gates], refs[2 * gates + 1 :]
    keep_ref, send_ref, hidden, weight_ref, back_ref, later_refs, x, down, sems = (*refs[:5], refs[5:-3], *refs[-3:])
    half = x.shape[1] // 2
    slots = x.shape[0]
    copies = []
    for i, (begin, size) in enumerate(spans):
        target = (down, *later_refs)[i // 2].at[:, pl.ds(i % 2 * size, size)]
        copies.append(pltpu.make_async_copy(down_hbm.at[:, pl.ds(begin, size)], target, sems.at[i]))
    for copy in copies:
        copy.start()

    expert = lax.rem(lax.axis_index("expert"), EXPERTS)
    pick_row = jnp.where(iota((slots, LANES), 1) == expert, 1.0, 0.0).astype(BF16)
    pick_col = jnp.where(iota((LANES, slots), 0) == expert, 1.0, 0.0).astype(BF16)

    def table(rank, packed_dim, slot_dim, first):
        at = iota(rank.shape, packed_dim) + first
        block = lax.div(at, 2 * rows)
        second = (at - block * (2 * rows)) >= rows
        hit = (rank > 0) & (iota(rank.shape, slot_dim) == block * CAP + rank.astype(jnp.int32) - 1)
        one = jnp.where(hit, 1.0, 0.0)
        return (jnp.where(second, 0.0, one).astype(BF16), jnp.where(second, one, 0.0).astype(BF16))

    first, left_x, right_x, slot_routing = 0, 0.0, 0.0, 0.0
    for ref in plane_refs:
        count = ref.shape[0]
        routing = ref[:, half:]
        rank_row = lax.dot_general(pick_row, routing, (((1,), (1,)), ((), ())), preferred_element_type=F32)
        rank_col = jnp.dot(routing, pick_col, preferred_element_type=F32)
        left, right = table(rank_row, 1, 0, first)
        back_left, back_right = table(rank_col, 0, 1, first)
        back_ref[first : first + count, :slots] = back_left
        back_ref[first : first + count, slots:] = back_right
        left_x = left_x + jnp.dot(left, ref[:, :half], preferred_element_type=F32)
        right_x = right_x + jnp.dot(right, ref[:, :half], preferred_element_type=F32)
        slot_routing = slot_routing + jnp.dot(left, routing, preferred_element_type=F32)
        first += count
    x[:, :half] = left_x.astype(BF16)
    x[:, half:] = right_x.astype(BF16)
    lane = iota(slot_routing.shape, 1)
    is_weight = (lax.rem(lane, EXPERTS) == expert) & (lane >= EXPERTS) & (lane < 4 * EXPERTS)
    weight = jnp.sum(jnp.where(is_weight, slot_routing, 0.0), axis=1, keepdims=True)
    weight_ref[...] = jnp.broadcast_to(weight, weight_ref.shape)

    at = 0
    for gate_ref, up_ref in zip(gate_refs, up_refs):
        units = gate_ref.shape[1]
        tile = 512 if units % 512 == 0 else units
        for i in range(units // tile):
            cols = slice(i * tile, (i + 1) * tile)
            gate_act = jnp.dot(x[...], gate_ref[:, cols], preferred_element_type=F32)
            up_act = jnp.dot(x[...], up_ref[:, cols], preferred_element_type=F32)
            hidden[:, at : at + tile] = (gate_act / (1.0 + jnp.exp(-gate_act)) * up_act).astype(BF16)
            at += tile
    for copy in copies[:2]:
        copy.wait()
    project(hidden[...], down, weight, back_ref[...], keep_ref, send_ref)
    for copy in copies[2:]:
        copy.wait()


def project_kernel(hidden, weight_ref, back, down, keep_ref, send_ref):
    project(hidden[...], down, weight_ref[:, :1], back[...], keep_ref, send_ref)


def body(tokens, expert_ids, gate_weights, w_gate, w_up, w_down):
    size = lax.axis_size("expert")
    steps = size // 4
    rows, width = tokens.shape
    units = w_gate.shape[2]
    half = width // 2
    block = 2 * rows
    count = size * block
    slots = size * CAP
    span = half // CHUNKS

    def send(x, pairs):
        return lax.ppermute(x, "expert", pairs)

    flip_core = [(i, i ^ 1) for i in range(size)]
    flip_second = [(i, i ^ 2) for i in range(size)]

    def shift(s):
        return [(i, (i + 4 * s) % size) for i in range(size)]

    own = pl.pallas_call(
        pack_kernel,
        out_shape=pltpu.VMEM((block, half + LANES), BF16),
        name="pack",
    )(tokens, expert_ids.T, gate_weights.T)
    gates = [load(w_gate[0], [(0, units)])]
    spans = [(c * span + h * half, span) for c in range(CHUNKS) for h in range(2)]

    shifted = [send(own, shift(s)) for s in range(1, steps)]
    across = send(own, flip_second)
    column = jnp.concatenate([own] + shifted, axis=0)
    column, across, gates[0] = lax.optimization_barrier((column, across, gates[0]))
    onward = column[block:]
    rest = send(onward, flip_second)
    column_of_core = send(column, flip_core)
    ups = [load(w_up[0], [(0, units)], onward)]
    second = jnp.concatenate([across, rest], axis=0)
    second, column_of_core, ups[0] = lax.optimization_barrier((second, column_of_core, ups[0]))
    plane = jnp.concatenate([column, second], axis=0)
    other = jnp.concatenate([column_of_core, send(second, flip_core)], axis=0)

    outs = [pltpu.VMEM((count // 2, span), BF16)] * 2
    keep, away, hidden, weight, back, *downs = pl.pallas_call(
        functools.partial(expert_kernel, rows, 2, len(gates), spans),
        out_shape=outs
        + [
            pltpu.VMEM((slots, units), BF16),
            pltpu.VMEM((slots, LANES), F32),
            pltpu.VMEM((count, 2 * slots), BF16),
        ]
        + [pltpu.VMEM((units, 2 * span), BF16)] * (CHUNKS - 1),
        in_specs=[IN_VMEM] * (2 + 2 * len(gates)) + [ANYWHERE],
        out_specs=[IN_VMEM] * (4 + CHUNKS),
        scratch_shapes=[
            pltpu.VMEM((slots, width), BF16),
            pltpu.VMEM((units, 2 * span), BF16),
            pltpu.SemaphoreType.DMA((len(spans),)),
        ],
        compiler_params=pltpu.CompilerParams(vmem_limit_bytes=10 * MIB),
        cost_estimate=pl.CostEstimate(
            flops=5 * slots * width * units, bytes_accessed=4 * width * units, transcendentals=slots * units
        ),
        name="experts",
    )(near(plane), near(other), *gates, *ups, far(w_down[0]))
    results = [(keep, away)]
    for down in downs:
        results.append(
            pl.pallas_call(
                project_kernel,
                out_shape=outs,
                in_specs=[IN_VMEM] * 4,
                out_specs=[IN_VMEM] * 2,
                compiler_params=pltpu.CompilerParams(vmem_limit_bytes=10 * MIB),
                cost_estimate=pl.CostEstimate(
                    flops=slots * width * units, bytes_accessed=width * units, transcendentals=0
                ),
                name="project",
            )(hidden, weight, back, down)
        )

    def add(a, b):
        return (a.astype(F32) + b.astype(F32)).astype(BF16)

    totals = []
    for keep, away in results:
        chip = add(keep, send(away, flip_core))
        line = add(chip[: count // 4], send(chip[count // 4 :], flip_second))
        total = line[:block].astype(F32)
        for s in range(1, steps):
            total = total + send(line[s * block : (s + 1) * block], shift(steps - s)).astype(F32)
        totals.append(total.astype(BF16))
    return jnp.concatenate([t[:rows] for t in totals] + [t[rows:] for t in totals], axis=1)


def solution(mesh):
    return jax.shard_map(
        body,
        mesh=mesh,
        in_specs=(
            P(("groups", "expert"), None),
            P(("groups", "expert"), None),
            P(("groups", "expert"), None),
            P("expert", None, None),
            P("expert", None, None),
            P("expert", None, None),
        ),
        out_specs=P(("groups", "expert"), None),
        check_vma=False,
    )
```

```python
import functools

import jax
import jax.numpy as jnp
from jax import lax
from jax.experimental import pallas as pl
from jax.experimental.pallas import tpu as pltpu
from jax.sharding import PartitionSpec as P

EXPERTS = 16
CAP = 8
LANES = 128
FIRST = 896
MIB = 1024 * 1024
BF16 = jnp.bfloat16
F32 = jnp.float32
IN_VMEM = pl.BlockSpec(memory_space=pltpu.VMEM)
ANYWHERE = pl.BlockSpec(memory_space=pl.ANY)


def iota(shape, dim):
    return lax.broadcasted_iota(jnp.int32, shape, dim)


def near(x):
    return pltpu.with_memory_space_constraint(x, pltpu.VMEM)


def far(x):
    return pltpu.with_memory_space_constraint(x, pltpu.HBM)


def pack_kernel(tokens_ref, ids_ref, weights_ref, out_ref):
    rows, width = tokens_ref.shape
    half = width // 2
    ids = ids_ref[...].T
    weights = weights_ref[...].T
    expert_of = lax.rem(iota((rows, LANES), 1), EXPERTS)
    kind = lax.div(iota((rows, LANES), 1), EXPERTS)
    chosen = jnp.zeros((rows, LANES), F32)
    weight = jnp.zeros((rows, LANES), F32)
    for j in range(ids.shape[1]):
        same = ids[:, j : j + 1] == expert_of
        chosen = chosen + jnp.where(same, 1.0, 0.0)
        weight = weight + jnp.where(same, weights[:, j : j + 1], 0.0)
    rank = jnp.zeros((rows, LANES), F32)
    row_of = iota((rows, LANES), 0)
    for r in range(rows - 1):
        rank = rank + jnp.where(row_of > r, chosen[r : r + 1, :], 0.0)
    high = weight.astype(BF16).astype(F32)
    middle = (weight - high).astype(BF16).astype(F32)
    low = weight - high - middle
    routing = jnp.where(
        kind == 0,
        chosen * (rank + 1.0),
        jnp.where(kind == 1, high, jnp.where(kind == 2, middle, jnp.where(kind == 3, low, 0.0))),
    )
    tokens = tokens_ref[...].astype(F32)
    out_ref[:, :half] = jnp.concatenate([tokens[:, :half], tokens[:, half:]], axis=0).astype(BF16)
    out_ref[:, half:] = jnp.concatenate([routing, routing], axis=0).astype(BF16)


def load_kernel(w_ref, *refs):
    out_ref, sem = refs[-2:]
    copy = pltpu.make_async_copy(w_ref, out_ref, sem)
    copy.start()
    copy.wait()


def load(w, *after):
    return pl.pallas_call(
        load_kernel,
        out_shape=pltpu.VMEM(w.shape, w.dtype),
        in_specs=[ANYWHERE] * (1 + len(after)),
        out_specs=IN_VMEM,
        scratch_shapes=[pltpu.SemaphoreType.DMA],
        compiler_params=pltpu.CompilerParams(vmem_limit_bytes=MIB),
        cost_estimate=pl.CostEstimate(flops=0, bytes_accessed=4 * w.size, transcendentals=0),
        name="load",
    )(far(w), *after)


def project(begin, hidden, down, weight, back, keep_ref, send_ref):
    span = keep_ref.shape[1]
    both = []
    half, units = down[0].shape[1] // 2, down[0].shape[0]
    for at in (begin, half + begin):
        act = 0.0
        for i, part in enumerate(down):
            act = act + jnp.dot(
                hidden[:, i * units : (i + 1) * units], part[:, at : at + span], preferred_element_type=F32
            )
        both.append((act * weight).astype(BF16))
    spread = jnp.dot(back, jnp.concatenate(both, axis=0), preferred_element_type=F32).astype(BF16)
    keep_ref[...] = spread[: keep_ref.shape[0]]
    send_ref[...] = spread[keep_ref.shape[0] :]


def expert_kernel(rows, planes, *refs):
    plane_refs, refs = refs[:planes], refs[planes:]
    gate, up, down_hbm, keep_ref, send_ref, hidden, weight_ref, back_ref, *down, x, sems = refs
    half = x.shape[1] // 2
    slots = x.shape[0]
    copies = [
        pltpu.make_async_copy(down_hbm.at[pl.ds(i * part.shape[0], part.shape[0])], part, sems.at[i])
        for i, part in enumerate(down)
    ]
    for copy in copies:
        copy.start()

    expert = lax.rem(lax.axis_index("expert"), EXPERTS)
    pick_row = jnp.where(iota((slots, LANES), 1) == expert, 1.0, 0.0).astype(BF16)
    pick_col = jnp.where(iota((LANES, slots), 0) == expert, 1.0, 0.0).astype(BF16)

    def table(rank, packed_dim, slot_dim, first):
        at = iota(rank.shape, packed_dim) + first
        block = lax.div(at, 2 * rows)
        second = (at - block * (2 * rows)) >= rows
        hit = (rank > 0) & (iota(rank.shape, slot_dim) == block * CAP + rank.astype(jnp.int32) - 1)
        one = jnp.where(hit, 1.0, 0.0)
        return (jnp.where(second, 0.0, one).astype(BF16), jnp.where(second, one, 0.0).astype(BF16))

    first, left_x, right_x, slot_routing = 0, 0.0, 0.0, 0.0
    for ref in plane_refs:
        count = ref.shape[0]
        routing = ref[:, half:]
        rank_row = lax.dot_general(pick_row, routing, (((1,), (1,)), ((), ())), preferred_element_type=F32)
        rank_col = jnp.dot(routing, pick_col, preferred_element_type=F32)
        left, right = table(rank_row, 1, 0, first)
        back_left, back_right = table(rank_col, 0, 1, first)
        back_ref[first : first + count, :slots] = back_left
        back_ref[first : first + count, slots:] = back_right
        left_x = left_x + jnp.dot(left, ref[:, :half], preferred_element_type=F32)
        right_x = right_x + jnp.dot(right, ref[:, :half], preferred_element_type=F32)
        slot_routing = slot_routing + jnp.dot(left, routing, preferred_element_type=F32)
        first += count
    x[:, :half] = left_x.astype(BF16)
    x[:, half:] = right_x.astype(BF16)
    lane = iota(slot_routing.shape, 1)
    is_weight = (lax.rem(lane, EXPERTS) == expert) & (lane >= EXPERTS) & (lane < 4 * EXPERTS)
    weight = jnp.sum(jnp.where(is_weight, slot_routing, 0.0), axis=1, keepdims=True)
    weight_ref[...] = jnp.broadcast_to(weight, weight_ref.shape)

    units = gate.shape[1]
    tile = 512 if units % 512 == 0 else units
    for i in range(units // tile):
        cols = slice(i * tile, (i + 1) * tile)
        gate_act = jnp.dot(x[...], gate[:, cols], preferred_element_type=F32)
        up_act = jnp.dot(x[...], up[:, cols], preferred_element_type=F32)
        hidden[:, cols] = (gate_act / (1.0 + jnp.exp(-gate_act)) * up_act).astype(BF16)
    for copy in copies:
        copy.wait()
    project(0, hidden, down, weight, back_ref[...], keep_ref, send_ref)


def project_kernel(begin, hidden, weight_ref, back, *refs):
    *down, keep_ref, send_ref = refs
    project(begin, hidden, down, weight_ref[:, :1], back[...], keep_ref, send_ref)


def body(tokens, expert_ids, gate_weights, w_gate, w_up, w_down):
    size = lax.axis_size("expert")
    steps = size // 4
    rows, width = tokens.shape
    units = w_gate.shape[2]
    half = width // 2
    block = 2 * rows
    grant = 3 * MIB + size * CAP * width * 4
    count = size * block
    slots = size * CAP
    widths = [FIRST, half - FIRST]

    def send(x, pairs):
        return lax.ppermute(x, "expert", pairs)

    flip_core = [(i, i ^ 1) for i in range(size)]
    flip_second = [(i, i ^ 2) for i in range(size)]

    def along(s, sign):
        if steps & (steps - 1) == 0:
            return [(i, i ^ (4 * s)) for i in range(size)]
        return [(i, (i + sign * 4 * s) % size) for i in range(size)]

    own = pl.pallas_call(
        pack_kernel,
        out_shape=pltpu.VMEM((block, half + LANES), BF16),
        name="pack",
    )(tokens, expert_ids.T, gate_weights.T)
    gate = load(w_gate[0])

    shifted = [send(own, along(s, 1)) for s in range(1, steps)]
    across = send(own, flip_second)
    column = jnp.concatenate([own] + shifted, axis=0)
    column, across, gate = lax.optimization_barrier((column, across, gate))
    onward = column[block:]
    rest = send(onward, flip_second)
    column_of_core = send(column, flip_core)
    up = load(w_up[0], onward)
    second = jnp.concatenate([across, rest], axis=0)
    second, column_of_core, up = lax.optimization_barrier((second, column_of_core, up))
    plane = jnp.concatenate([column, second], axis=0)
    other = jnp.concatenate([column_of_core, send(second, flip_core)], axis=0)

    outs = [[pltpu.VMEM((count // 2, span), BF16)] * 2 for span in widths]
    keep, away, hidden, weight, back, *down = pl.pallas_call(
        functools.partial(expert_kernel, rows, 2),
        out_shape=outs[0]
        + [
            pltpu.VMEM((slots, units), BF16),
            pltpu.VMEM((slots, LANES), F32),
            pltpu.VMEM((count, 2 * slots), BF16),
        ]
        + [pltpu.VMEM((units // 2, width), BF16)] * 2,
        in_specs=[IN_VMEM] * 4 + [ANYWHERE],
        out_specs=[IN_VMEM] * 7,
        scratch_shapes=[pltpu.VMEM((slots, width), BF16), pltpu.SemaphoreType.DMA((2,))],
        compiler_params=pltpu.CompilerParams(vmem_limit_bytes=grant),
        cost_estimate=pl.CostEstimate(
            flops=5 * slots * width * units, bytes_accessed=4 * width * units, transcendentals=slots * units
        ),
        name="experts",
    )(near(plane), near(other), gate, up, far(w_down[0]))
    later = pl.pallas_call(
        functools.partial(project_kernel, widths[0]),
        out_shape=outs[1],
        in_specs=[IN_VMEM] * 5,
        out_specs=[IN_VMEM] * 2,
        compiler_params=pltpu.CompilerParams(vmem_limit_bytes=grant),
        cost_estimate=pl.CostEstimate(flops=slots * width * units, bytes_accessed=width * units, transcendentals=0),
        name="project",
    )(hidden, weight, back, *down)

    def add(a, b):
        return (a.astype(F32) + b.astype(F32)).astype(BF16)

    chips = [add(keep, send(away, flip_core)), add(later[0], send(later[1], flip_core))]
    totals = []
    for chip in chips:
        line = add(chip[: count // 4], send(chip[count // 4 :], flip_second))
        total = line[:block].astype(F32)
        for s in range(1, steps):
            total = total + send(line[s * block : (s + 1) * block], along(s, -1)).astype(F32)
        totals.append(total.astype(BF16))
    return jnp.concatenate([t[:rows] for t in totals] + [t[rows:] for t in totals], axis=1)


def solution(mesh):
    return jax.shard_map(
        body,
        mesh=mesh,
        in_specs=(
            P(("groups", "expert"), None),
            P(("groups", "expert"), None),
            P(("groups", "expert"), None),
            P("expert", None, None),
            P("expert", None, None),
            P("expert", None, None),
        ),
        out_specs=P(("groups", "expert"), None),
        check_vma=False,
    )
```

```python
import functools

import jax
import jax.numpy as jnp
from jax import lax
from jax.experimental import pallas as pl
from jax.experimental.pallas import tpu as pltpu
from jax.sharding import PartitionSpec as P

EXPERTS = 16
CAP = 8
LANES = 128
FIRST = 896
MIB = 1024 * 1024
BF16 = jnp.bfloat16
F32 = jnp.float32
IN_VMEM = pl.BlockSpec(memory_space=pltpu.VMEM)
ANYWHERE = pl.BlockSpec(memory_space=pl.ANY)


def iota(shape, dim):
    return lax.broadcasted_iota(jnp.int32, shape, dim)


def near(x):
    return pltpu.with_memory_space_constraint(x, pltpu.VMEM)


def far(x):
    return pltpu.with_memory_space_constraint(x, pltpu.HBM)


def pack_kernel(tokens_ref, ids_ref, weights_ref, out_ref):
    rows, width = tokens_ref.shape
    half = width // 2
    ids = ids_ref[...].T
    weights = weights_ref[...].T
    expert_of = lax.rem(iota((rows, LANES), 1), EXPERTS)
    kind = lax.div(iota((rows, LANES), 1), EXPERTS)
    chosen = jnp.zeros((rows, LANES), F32)
    weight = jnp.zeros((rows, LANES), F32)
    for j in range(ids.shape[1]):
        same = ids[:, j : j + 1] == expert_of
        chosen = chosen + jnp.where(same, 1.0, 0.0)
        weight = weight + jnp.where(same, weights[:, j : j + 1], 0.0)
    rank = jnp.zeros((rows, LANES), F32)
    row_of = iota((rows, LANES), 0)
    for r in range(rows - 1):
        rank = rank + jnp.where(row_of > r, chosen[r : r + 1, :], 0.0)
    high = weight.astype(BF16).astype(F32)
    middle = (weight - high).astype(BF16).astype(F32)
    low = weight - high - middle
    routing = jnp.where(
        kind == 0,
        chosen * (rank + 1.0),
        jnp.where(kind == 1, high, jnp.where(kind == 2, middle, jnp.where(kind == 3, low, 0.0))),
    )
    tokens = tokens_ref[...].astype(F32)
    out_ref[:, :half] = jnp.concatenate([tokens[:, :half], tokens[:, half:]], axis=0).astype(BF16)
    out_ref[:, half:] = jnp.concatenate([routing, routing], axis=0).astype(BF16)


def load_kernel(w_ref, *refs):
    out_ref, sem = refs[-2:]
    copy = pltpu.make_async_copy(w_ref, out_ref, sem)
    copy.start()
    copy.wait()


def load(w, *after):
    return pl.pallas_call(
        load_kernel,
        out_shape=pltpu.VMEM(w.shape, w.dtype),
        in_specs=[ANYWHERE] * (1 + len(after)),
        out_specs=IN_VMEM,
        scratch_shapes=[pltpu.SemaphoreType.DMA],
        compiler_params=pltpu.CompilerParams(vmem_limit_bytes=MIB),
        cost_estimate=pl.CostEstimate(flops=0, bytes_accessed=4 * w.size, transcendentals=0),
        name="load",
    )(far(w), *after)


def project(begin, hidden, down, weight, back, keep_ref, send_ref):
    span = keep_ref.shape[1]
    both = []
    half, units = down[0].shape[1] // 2, down[0].shape[0]
    for at in (begin, half + begin):
        act = 0.0
        for i, part in enumerate(down):
            act = act + jnp.dot(
                hidden[:, i * units : (i + 1) * units], part[:, at : at + span], preferred_element_type=F32
            )
        both.append((act * weight).astype(BF16))
    spread = jnp.dot(back, jnp.concatenate(both, axis=0), preferred_element_type=F32).astype(BF16)
    keep_ref[...] = spread[: keep_ref.shape[0]]
    send_ref[...] = spread[keep_ref.shape[0] :]


def expert_kernel(rows, planes, *refs):
    plane_refs, refs = refs[:planes], refs[planes:]
    gate, up, down_hbm, keep_ref, send_ref, hidden, weight_ref, back_ref, *down, x, sems = refs
    half = x.shape[1] // 2
    slots = x.shape[0]
    copies = [
        pltpu.make_async_copy(down_hbm.at[pl.ds(i * part.shape[0], part.shape[0])], part, sems.at[i])
        for i, part in enumerate(down)
    ]
    for copy in copies:
        copy.start()

    expert = lax.rem(lax.axis_index("expert"), EXPERTS)
    pick_row = jnp.where(iota((slots, LANES), 1) == expert, 1.0, 0.0).astype(BF16)
    pick_col = jnp.where(iota((LANES, slots), 0) == expert, 1.0, 0.0).astype(BF16)

    def table(rank, packed_dim, slot_dim, first):
        at = iota(rank.shape, packed_dim) + first
        block = lax.div(at, 2 * rows)
        second = (at - block * (2 * rows)) >= rows
        hit = (rank > 0) & (iota(rank.shape, slot_dim) == block * CAP + rank.astype(jnp.int32) - 1)
        one = jnp.where(hit, 1.0, 0.0)
        return (jnp.where(second, 0.0, one).astype(BF16), jnp.where(second, one, 0.0).astype(BF16))

    first, left_x, right_x, slot_routing = 0, 0.0, 0.0, 0.0
    for ref in plane_refs:
        count = ref.shape[0]
        routing = ref[:, half:]
        rank_row = lax.dot_general(pick_row, routing, (((1,), (1,)), ((), ())), preferred_element_type=F32)
        rank_col = jnp.dot(routing, pick_col, preferred_element_type=F32)
        left, right = table(rank_row, 1, 0, first)
        back_left, back_right = table(rank_col, 0, 1, first)
        back_ref[first : first + count, :slots] = back_left
        back_ref[first : first + count, slots:] = back_right
        left_x = left_x + jnp.dot(left, ref[:, :half], preferred_element_type=F32)
        right_x = right_x + jnp.dot(right, ref[:, :half], preferred_element_type=F32)
        slot_routing = slot_routing + jnp.dot(left, routing, preferred_element_type=F32)
        first += count
    x[:, :half] = left_x.astype(BF16)
    x[:, half:] = right_x.astype(BF16)
    lane = iota(slot_routing.shape, 1)
    is_weight = (lax.rem(lane, EXPERTS) == expert) & (lane >= EXPERTS) & (lane < 4 * EXPERTS)
    weight = jnp.sum(jnp.where(is_weight, slot_routing, 0.0), axis=1, keepdims=True)
    weight_ref[...] = jnp.broadcast_to(weight, weight_ref.shape)

    units = gate.shape[1]
    tile = 512 if units % 512 == 0 else units
    for i in range(units // tile):
        cols = slice(i * tile, (i + 1) * tile)
        gate_act = jnp.dot(x[...], gate[:, cols], preferred_element_type=F32)
        up_act = jnp.dot(x[...], up[:, cols], preferred_element_type=F32)
        hidden[:, cols] = (gate_act / (1.0 + jnp.exp(-gate_act)) * up_act).astype(BF16)
    for copy in copies:
        copy.wait()
    project(0, hidden, down, weight, back_ref[...], keep_ref, send_ref)


def project_kernel(begin, hidden, weight_ref, back, *refs):
    *down, keep_ref, send_ref = refs
    project(begin, hidden, down, weight_ref[:, :1], back[...], keep_ref, send_ref)


def body(tokens, expert_ids, gate_weights, w_gate, w_up, w_down):
    size = lax.axis_size("expert")
    steps = size // 4
    rows, width = tokens.shape
    units = w_gate.shape[2]
    half = width // 2
    block = 2 * rows
    grant = 3 * MIB + size * CAP * width * 4
    count = size * block
    slots = size * CAP
    widths = [FIRST, half - FIRST]

    def send(x, pairs):
        return lax.ppermute(x, "expert", pairs)

    flip_core = [(i, i ^ 1) for i in range(size)]
    flip_second = [(i, i ^ 2) for i in range(size)]

    def along(s):
        return [(i, i ^ (4 * s)) for i in range(size)]

    own = pl.pallas_call(
        pack_kernel,
        out_shape=pltpu.VMEM((block, half + LANES), BF16),
        name="pack",
    )(tokens, expert_ids.T, gate_weights.T)
    gate = load(w_gate[0])

    order, bits = [0], []
    while len(order) < steps:
        bits.append(len(order))
        order = [2 * s for s in order] + [2 * s + 1 for s in order]
    shifted = [send(own, along(s)) for s in order[1:]]
    across = send(own, flip_second)
    column = jnp.concatenate([own] + shifted, axis=0)
    column, across, gate = lax.optimization_barrier((column, across, gate))
    onward = column[block:]
    rest = send(onward, flip_second)
    column_of_core = send(column, flip_core)
    up = load(w_up[0], onward)
    second = jnp.concatenate([across, rest], axis=0)
    second, column_of_core, up = lax.optimization_barrier((second, column_of_core, up))
    plane = jnp.concatenate([column, second], axis=0)
    other = jnp.concatenate([column_of_core, send(second, flip_core)], axis=0)

    outs = [[pltpu.VMEM((count // 2, span), BF16)] * 2 for span in widths]
    keep, away, hidden, weight, back, *down = pl.pallas_call(
        functools.partial(expert_kernel, rows, 2),
        out_shape=outs[0]
        + [
            pltpu.VMEM((slots, units), BF16),
            pltpu.VMEM((slots, LANES), F32),
            pltpu.VMEM((count, 2 * slots), BF16),
        ]
        + [pltpu.VMEM((units // 2, width), BF16)] * 2,
        in_specs=[IN_VMEM] * 4 + [ANYWHERE],
        out_specs=[IN_VMEM] * 7,
        scratch_shapes=[pltpu.VMEM((slots, width), BF16), pltpu.SemaphoreType.DMA((2,))],
        compiler_params=pltpu.CompilerParams(vmem_limit_bytes=grant),
        cost_estimate=pl.CostEstimate(
            flops=5 * slots * width * units, bytes_accessed=4 * width * units, transcendentals=slots * units
        ),
        name="experts",
    )(near(plane), near(other), gate, up, far(w_down[0]))
    later = pl.pallas_call(
        functools.partial(project_kernel, widths[0]),
        out_shape=outs[1],
        in_specs=[IN_VMEM] * 5,
        out_specs=[IN_VMEM] * 2,
        compiler_params=pltpu.CompilerParams(vmem_limit_bytes=grant),
        cost_estimate=pl.CostEstimate(flops=slots * width * units, bytes_accessed=width * units, transcendentals=0),
        name="project",
    )(hidden, weight, back, *down)

    def add(a, b):
        return (a.astype(F32) + b.astype(F32)).astype(BF16)

    chips = [add(keep, send(away, flip_core)), add(later[0], send(later[1], flip_core))]
    def halve(total, parts, pairs):
        span = total.shape[1]
        total = total.reshape(parts, 2, -1, span)
        kept, given = total[:, 0].reshape(-1, span), total[:, 1].reshape(-1, span)
        return add(kept, send(given, pairs))

    first, second = chips
    steps_of_first = [(1, flip_second)] + [(1, along(bit)) for bit in bits]
    steps_of_second = [(2, along(bit)) for bit in bits] + [(1, flip_second)]
    for (parts, pairs), (other_parts, other_pairs) in zip(steps_of_first, steps_of_second):
        first = halve(first, parts, pairs)
        second = halve(second, other_parts, other_pairs)
    return jnp.concatenate([first[:rows], second[:rows], first[rows:], second[rows:]], axis=1)


def solution(mesh):
    return jax.shard_map(
        body,
        mesh=mesh,
        in_specs=(
            P(("groups", "expert"), None),
            P(("groups", "expert"), None),
            P(("groups", "expert"), None),
            P("expert", None, None),
            P("expert", None, None),
            P("expert", None, None),
        ),
        out_specs=P(("groups", "expert"), None),
        check_vma=False,
    )
```

```python
import functools

import jax
import jax.numpy as jnp
from jax import lax
from jax.experimental import pallas as pl
from jax.experimental.pallas import tpu as pltpu
from jax.sharding import PartitionSpec as P

EXPERTS = 16
CAP = 8
LANES = 128
FIRST = 896
MIB = 1024 * 1024
BF16 = jnp.bfloat16
F32 = jnp.float32
IN_VMEM = pl.BlockSpec(memory_space=pltpu.VMEM)
ANYWHERE = pl.BlockSpec(memory_space=pl.ANY)


def iota(shape, dim):
    return lax.broadcasted_iota(jnp.int32, shape, dim)


def near(x):
    return pltpu.with_memory_space_constraint(x, pltpu.VMEM)


def far(x):
    return pltpu.with_memory_space_constraint(x, pltpu.HBM)


def pack_kernel(tokens_ref, ids_ref, weights_ref, out_ref):
    rows, width = tokens_ref.shape
    half = width // 2
    ids = ids_ref[...].T
    weights = weights_ref[...].T
    expert_of = lax.rem(iota((rows, LANES), 1), EXPERTS)
    kind = lax.div(iota((rows, LANES), 1), EXPERTS)
    chosen = jnp.zeros((rows, LANES), F32)
    weight = jnp.zeros((rows, LANES), F32)
    for j in range(ids.shape[1]):
        same = ids[:, j : j + 1] == expert_of
        chosen = chosen + jnp.where(same, 1.0, 0.0)
        weight = weight + jnp.where(same, weights[:, j : j + 1], 0.0)
    rank = jnp.zeros((rows, LANES), F32)
    row_of = iota((rows, LANES), 0)
    for r in range(rows - 1):
        rank = rank + jnp.where(row_of > r, chosen[r : r + 1, :], 0.0)
    high = weight.astype(BF16).astype(F32)
    middle = (weight - high).astype(BF16).astype(F32)
    low = weight - high - middle
    routing = jnp.where(
        kind == 0,
        chosen * (rank + 1.0),
        jnp.where(kind == 1, high, jnp.where(kind == 2, middle, jnp.where(kind == 3, low, 0.0))),
    )
    tokens = tokens_ref[...].astype(F32)
    out_ref[:, :half] = jnp.concatenate([tokens[:, :half], tokens[:, half:]], axis=0).astype(BF16)
    out_ref[:, half:] = jnp.concatenate([routing, routing], axis=0).astype(BF16)


def load_kernel(w_ref, *refs):
    out_ref, sem = refs[-2:]
    copy = pltpu.make_async_copy(w_ref, out_ref, sem)
    copy.start()
    copy.wait()


def load(w, *after):
    return pl.pallas_call(
        load_kernel,
        out_shape=pltpu.VMEM(w.shape, w.dtype),
        in_specs=[ANYWHERE] * (1 + len(after)),
        out_specs=IN_VMEM,
        scratch_shapes=[pltpu.SemaphoreType.DMA],
        compiler_params=pltpu.CompilerParams(vmem_limit_bytes=MIB),
        cost_estimate=pl.CostEstimate(flops=0, bytes_accessed=4 * w.size, transcendentals=0),
        name="load",
    )(far(w), *after)


def project(begin, hidden, down, weight, back, keep_ref, send_ref):
    span = keep_ref.shape[1]
    both = []
    half, units = down[0].shape[1] // 2, down[0].shape[0]
    for at in (begin, half + begin):
        act = 0.0
        for i, part in enumerate(down):
            act = act + jnp.dot(
                hidden[:, i * units : (i + 1) * units], part[:, at : at + span], preferred_element_type=F32
            )
        both.append((act * weight).astype(BF16))
    spread = jnp.dot(back, jnp.concatenate(both, axis=0), preferred_element_type=F32).astype(BF16)
    keep_ref[...] = spread[: keep_ref.shape[0]]
    send_ref[...] = spread[keep_ref.shape[0] :]


def expert_kernel(rows, planes, *refs):
    plane_refs, refs = refs[:planes], refs[planes:]
    gate, up, down_hbm, keep_ref, send_ref, hidden, weight_ref, back_ref, *down, x, sems = refs
    half = x.shape[1] // 2
    slots = x.shape[0]
    copies = [
        pltpu.make_async_copy(down_hbm.at[pl.ds(i * part.shape[0], part.shape[0])], part, sems.at[i])
        for i, part in enumerate(down)
    ]
    for copy in copies:
        copy.start()

    expert = lax.rem(lax.axis_index("expert"), EXPERTS)
    pick_row = jnp.where(iota((slots, LANES), 1) == expert, 1.0, 0.0).astype(BF16)
    pick_col = jnp.where(iota((LANES, slots), 0) == expert, 1.0, 0.0).astype(BF16)

    def table(rank, packed_dim, slot_dim, first):
        at = iota(rank.shape, packed_dim) + first
        block = lax.div(at, 2 * rows)
        second = (at - block * (2 * rows)) >= rows
        hit = (rank > 0) & (iota(rank.shape, slot_dim) == block * CAP + rank.astype(jnp.int32) - 1)
        one = jnp.where(hit, 1.0, 0.0)
        return (jnp.where(second, 0.0, one).astype(BF16), jnp.where(second, one, 0.0).astype(BF16))

    first, left_x, right_x, slot_routing = 0, 0.0, 0.0, 0.0
    for ref in plane_refs:
        count = ref.shape[0]
        routing = ref[:, half:]
        rank_row = lax.dot_general(pick_row, routing, (((1,), (1,)), ((), ())), preferred_element_type=F32)
        rank_col = jnp.dot(routing, pick_col, preferred_element_type=F32)
        left, right = table(rank_row, 1, 0, first)
        back_left, back_right = table(rank_col, 0, 1, first)
        back_ref[first : first + count, :slots] = back_left
        back_ref[first : first + count, slots:] = back_right
        left_x = left_x + jnp.dot(left, ref[:, :half], preferred_element_type=F32)
        right_x = right_x + jnp.dot(right, ref[:, :half], preferred_element_type=F32)
        slot_routing = slot_routing + jnp.dot(left, routing, preferred_element_type=F32)
        first += count
    x[:, :half] = left_x.astype(BF16)
    x[:, half:] = right_x.astype(BF16)
    lane = iota(slot_routing.shape, 1)
    is_weight = (lax.rem(lane, EXPERTS) == expert) & (lane >= EXPERTS) & (lane < 4 * EXPERTS)
    weight = jnp.sum(jnp.where(is_weight, slot_routing, 0.0), axis=1, keepdims=True)
    weight_ref[...] = jnp.broadcast_to(weight, weight_ref.shape)

    units = gate.shape[1]
    tile = 512 if units % 512 == 0 else units
    for i in range(units // tile):
        cols = slice(i * tile, (i + 1) * tile)
        gate_act = jnp.dot(x[...], gate[:, cols], preferred_element_type=F32)
        up_act = jnp.dot(x[...], up[:, cols], preferred_element_type=F32)
        hidden[:, cols] = (gate_act / (1.0 + jnp.exp(-gate_act)) * up_act).astype(BF16)
    for copy in copies:
        copy.wait()
    project(0, hidden, down, weight, back_ref[...], keep_ref, send_ref)


def project_kernel(begin, hidden, weight_ref, back, *refs):
    *down, keep_ref, send_ref = refs
    project(begin, hidden, down, weight_ref[:, :1], back[...], keep_ref, send_ref)


def body(tokens, expert_ids, gate_weights, w_gate, w_up, w_down):
    size = lax.axis_size("expert")
    steps = size // 4
    rows, width = tokens.shape
    units = w_gate.shape[2]
    half = width // 2
    block = 2 * rows
    grant = 3 * MIB + size * CAP * width * 4
    count = size * block
    slots = size * CAP
    widths = [FIRST, half - FIRST]

    def send(x, pairs):
        return lax.ppermute(x, "expert", pairs)

    flip_core = [(i, i ^ 1) for i in range(size)]
    flip_second = [(i, i ^ 2) for i in range(size)]

    def along(s, sign):
        if steps & (steps - 1) == 0:
            return [(i, i ^ (4 * s)) for i in range(size)]
        return [(i, (i + sign * 4 * s) % size) for i in range(size)]

    own = pl.pallas_call(
        pack_kernel,
        out_shape=pltpu.VMEM((block, half + LANES), BF16),
        name="pack",
    )(tokens, expert_ids.T, gate_weights.T)
    gate = load(w_gate[0])

    shifted = [send(own, along(s, 1)) for s in range(1, steps)]
    across = send(own, flip_second)
    column = jnp.concatenate([own] + shifted, axis=0)
    column, across, gate = lax.optimization_barrier((column, across, gate))
    onward = column[block:]
    rest = send(onward, flip_second)
    column_of_core = send(column, flip_core)
    up = load(w_up[0], onward)
    second = jnp.concatenate([across, rest], axis=0)
    second, column_of_core, up = lax.optimization_barrier((second, column_of_core, up))
    plane = jnp.concatenate([column, second], axis=0)
    other = jnp.concatenate([column_of_core, send(second, flip_core)], axis=0)

    outs = [[pltpu.VMEM((count // 2, span), BF16)] * 2 for span in widths]
    keep, away, hidden, weight, back, *down = pl.pallas_call(
        functools.partial(expert_kernel, rows, 2),
        out_shape=outs[0]
        + [
            pltpu.VMEM((slots, units), BF16),
            pltpu.VMEM((slots, LANES), F32),
            pltpu.VMEM((count, 2 * slots), BF16),
        ]
        + [pltpu.VMEM((units // 2, width), BF16)] * 2,
        in_specs=[IN_VMEM] * 4 + [ANYWHERE],
        out_specs=[IN_VMEM] * 7,
        scratch_shapes=[pltpu.VMEM((slots, width), BF16), pltpu.SemaphoreType.DMA((2,))],
        compiler_params=pltpu.CompilerParams(vmem_limit_bytes=grant),
        cost_estimate=pl.CostEstimate(
            flops=5 * slots * width * units, bytes_accessed=4 * width * units, transcendentals=slots * units
        ),
        name="experts",
    )(near(plane), near(other), gate, up, far(w_down[0]))
    later = pl.pallas_call(
        functools.partial(project_kernel, widths[0]),
        out_shape=outs[1],
        in_specs=[IN_VMEM] * 5,
        out_specs=[IN_VMEM] * 2,
        compiler_params=pltpu.CompilerParams(vmem_limit_bytes=grant),
        cost_estimate=pl.CostEstimate(flops=slots * width * units, bytes_accessed=width * units, transcendentals=0),
        name="project",
    )(hidden, weight, back, *down)

    def add(a, b):
        return (a.astype(F32) + b.astype(F32)).astype(BF16)

    chips = [add(keep, send(away, flip_core)), add(later[0], send(later[1], flip_core))]
    totals = []
    for chip in chips:
        line = add(chip[: count // 4], send(chip[count // 4 :], flip_second))
        total = line[:block].astype(F32)
        for s in range(steps - 1, 0, -1):
            total = total + send(line[s * block : (s + 1) * block], along(s, -1)).astype(F32)
        totals.append(total.astype(BF16))
    return jnp.concatenate([t[:rows] for t in totals] + [t[rows:] for t in totals], axis=1)


def solution(mesh):
    return jax.shard_map(
        body,
        mesh=mesh,
        in_specs=(
            P(("groups", "expert"), None),
            P(("groups", "expert"), None),
            P(("groups", "expert"), None),
            P("expert", None, None),
            P("expert", None, None),
            P("expert", None, None),
        ),
        out_specs=P(("groups", "expert"), None),
        check_vma=False,
    )
```
